32 devices in a mesh: dp: 8 (over z, x), context: 4 (over y, core).
Axes of the slice: x: 2, y: 2, z: 4, core: 2. Of those that a mesh axis runs over, the one named last changes fastest.
Arguments:
- values: bfloat16 [1024, 4096], P('context', 'dp'), may hold values from -6 to 6
- gates: bfloat16 [1024, 4096], P('context', 'dp'), may hold values from -6 to 6
- filters: float32 [1024, 512], P('context'), may hold values from -6 to 6
- skips: float32 [4096], P('dp'), may hold values from 0.5 to 1.5
- grad_out: bfloat16 [1024, 4096], P('context', 'dp'), may hold values from -6 to 6
Outputs:
- mixed: bfloat16 [1024, 4096], P('context', 'dp')
- grad_gates: bfloat16 [1024, 4096], P('context', 'dp')
- grad_values: bfloat16 [1024, 4096], P('context', 'dp')
- grad_filters: float32 [1024, 512], P('context')
The draws below stay inside these ranges and needn't reach their ends.
All inputs are finite; a program needn't handle non-finite values.
Results may differ from the reference program's by a relative error of at most 0.001.
Values may be sent and summed in bfloat16 or wider, within the bound.
A program may use at most 128 MiB of HBM per device.

```python
import math
import jax
import jax.numpy as jnp
from jax import lax

CH = 4096
LENGTH = 1024
GROUPS = 512
N_DP = 8


def level_of(stream_key, shape, cuts, low, high):
    level = 1.0
    for dim, shards_of in cuts:
        draws = jax.random.uniform(jax.random.fold_in(jax.random.fold_in(stream_key, 6), dim), (shards_of,), jnp.float32, low / len(cuts), high / len(cuts))
        level = level * jnp.repeat(jnp.exp(draws), shape[dim] // shards_of).reshape((-1,) + (1,) * (len(shape) - 1 - dim))
    return level


def centred(rng, dims, width, reach, pieces=(), held_as=jnp.bfloat16):
    factor_of = level_of(rng, dims, pieces, -0.22, 0.18) if pieces else 1.0
    result = jax.random.normal(rng, dims, jnp.float32) * width * factor_of
    return jnp.minimum(jnp.maximum(result, -reach), reach).astype(held_as)


def setup_inputs(seed: int = 0) -> dict:
    key_of = jax.random.split(jax.random.key(seed), 6)
    return {
        "values": centred(key_of[0], (LENGTH, CH), 1.0, 6.0, ((0, 4), (1, 8))),
        "gates": centred(key_of[1], (LENGTH, CH), 1.0, 6.0, ((0, 4), (1, 8))),
        "filters": centred(key_of[2], (LENGTH, GROUPS), 1.0, 6.0, ((0, 4),), jnp.float32),
        "skips": jnp.clip(0.5 + 1.0 * jax.random.uniform(key_of[3], (CH,), jnp.float32) ** level_of(key_of[3], (CH,), ((0, 8),), -0.2, 0.2), 0.5, 1.5),
        "grad_out": centred(key_of[4], (LENGTH, CH), 1.0, 6.0, ((0, 4), (1, 8))),
    }


def reference(values, gates, filters, skips, grad_out):
    padded = 2 * LENGTH
    scale = 1.0 / math.sqrt(LENGTH)
    filter_spec = jnp.fft.rfft(filters, n=padded, axis=0)

    def one_block(index):
        start = index * GROUPS
        value_cols = lax.dynamic_slice_in_dim(values, start, GROUPS, 1).astype(jnp.float32)
        gate_cols = lax.dynamic_slice_in_dim(gates, start, GROUPS, 1).astype(jnp.float32)
        grad_cols = lax.dynamic_slice_in_dim(grad_out, start, GROUPS, 1).astype(jnp.float32)
        skip_cols = lax.dynamic_slice_in_dim(skips, start, GROUPS, 0)
        value_spec = jnp.fft.rfft(value_cols, n=padded, axis=0)
        conv = jnp.fft.irfft(value_spec * filter_spec, n=padded, axis=0)[:LENGTH] * scale
        mixer = conv + skip_cols * value_cols
        mixed = (gate_cols * mixer).astype(jnp.bfloat16)
        grad_gate = (grad_cols * mixer).astype(jnp.bfloat16)
        grad_mixer = grad_cols * gate_cols
        grad_spec = jnp.fft.rfft(grad_mixer, n=padded, axis=0)
        back = jnp.fft.irfft(grad_spec * jnp.conj(filter_spec), n=padded, axis=0)[:LENGTH] * scale
        grad_value = (back + skip_cols * grad_mixer).astype(jnp.bfloat16)
        grad_filter = jnp.fft.irfft(grad_spec * jnp.conj(value_spec), n=padded, axis=0)[:LENGTH] * scale
        return (mixed, grad_gate, grad_value, grad_filter)
    results = lax.map(one_block, jnp.arange(N_DP, dtype=jnp.int32))

    def columns(stacked):
        return jnp.moveaxis(stacked, 0, 1).reshape(LENGTH, CH)
    return (columns(results[0]), columns(results[1]), columns(results[2]), lax.optimization_barrier(jnp.sum(results[3], axis=0)))
```

```python
from functools import partial
import math

import jax
import jax.numpy as jnp
import numpy as np
from jax import lax
from jax.experimental import pallas as pl
from jax.experimental.pallas import tpu as pltpu
from jax.sharding import PartitionSpec as P

LANES = 128
STRIP = 16


def plan(length):
    inner = 128
    while 2 * length // inner > 32:
        inner *= 2
    return 2 * length // inner, inner


def tables(length):
    outer, inner = plan(length)
    total = 2 * length
    pos = np.arange(inner, dtype=np.int64)[None, :]
    freq = np.arange(inner, dtype=np.int64)[:, None]
    fwd, inv = [], []
    for k in range(outer // 2 + 1):
        angle = -2.0 * np.pi / total * ((pos * (k + outer * freq)) % total)
        c, s = np.cos(angle), np.sin(angle)
        m = np.block([[c, -s], [s, c]])
        fwd.append(m)
        weight = (1.0 if k in (0, outer // 2) else 1.0) / total / math.sqrt(length)
        inv.append(m.T * weight)

    def split(stack):
        full = np.stack(stack).astype(np.float32)
        hi = full.astype(jnp.bfloat16)
        lo = (full - hi.astype(np.float32)).astype(jnp.bfloat16)
        return hi, lo

    return split(fwd) + split(inv)


def add(a, b):
    if a is None:
        return b
    return a if b is None else a + b


def sub(a, b):
    if b is None:
        return a
    return -b if a is None else a - b


def rotate(z, turn):
    re, im = z
    eighth = round(turn * 8) % 8 if abs(turn * 8 - round(turn * 8)) < 1e-9 else None
    if eighth == 0:
        return z
    if eighth == 4:
        return sub(None, re) if re is not None else None, sub(None, im) if im is not None else None
    if eighth == 2:
        return (None if im is None else -im), re
    if eighth == 6:
        return im, (None if re is None else -re)
    c, s = math.cos(2 * math.pi * turn), math.sin(2 * math.pi * turn)
    if im is None:
        return (None, None) if re is None else (re * c, re * s)
    if re is None:
        return im * -s, im * c
    if eighth is not None:
        if eighth == 1:
            return (re - im) * c, (re + im) * c
        if eighth == 3:
            return (re + im) * c, (im - re) * -c
        if eighth == 5:
            return (re - im) * c, (re + im) * c
        return (re + im) * c, (im - re) * c
    return re * c - im * s, re * s + im * c


def real_dft(xs):
    n = len(xs)
    if n == 1:
        return [(xs[0], None)]
    even, odd = real_dft(xs[::2]), real_dft(xs[1::2])
    out = [None] * (n // 2 + 1)
    for k in range(n // 4 + 1):
        er, ei = even[k]
        rr, ri = rotate(odd[k], -k / n)
        out[k] = (add(er, rr), add(ei, ri))
        if n // 2 - k != k:
            dr, di = sub(er, rr), sub(ei, ri)
            out[n // 2 - k] = (dr, None if di is None else -di)
    return out


def real_inverse(hs):
    n = 2 * (len(hs) - 1)
    if n == 2:
        return [add(hs[0][0], hs[1][0])]
    even, odd = [], []
    for k in range(n // 4 + 1):
        ar, ai = hs[k]
        br, bi = hs[n // 2 - k]
        if k == n // 4:
            even.append((ar + ar, None))
            odd.append((-(ai + ai), None))
            continue
        even.append((add(ar, br), sub(ai, bi)))
        odd.append(rotate((sub(ar, br), add(ai, bi)), k / n))
    out = [None] * (n // 2)
    out[::2] = real_inverse(even)
    out[1::2] = real_inverse(odd)
    return out


def split_store(hi_ref, lo_ref, index, value):
    hi = value.astype(jnp.bfloat16)
    hi_ref[index] = hi
    lo_ref[index] = (value - hi.astype(jnp.float32)).astype(jnp.bfloat16)


def split(value):
    hi = value.astype(jnp.bfloat16)
    return hi, (value - hi.astype(jnp.float32)).astype(jnp.bfloat16)


def dot3(mat_hi, mat_lo, hi, lo):
    dot = partial(jnp.dot, preferred_element_type=jnp.float32)
    return dot(mat_hi, hi) + dot(mat_hi, lo) + dot(mat_lo, hi)


def local_kernel(outer, inner, v_ref, g_ref, o_ref, f_ref, s_ref, fh, fl, ih, il,
                 mixed_ref, ggate_ref, gval_ref, gfil_ref, ahi, alo, back):
    half = outer // 2
    width = v_ref.shape[1]
    k = pl.program_id(0)

    def spread(strip, _):
        row = pl.multiple_of(strip * STRIP, STRIP)

        def take(ref, a):
            return ref[pl.ds(pl.multiple_of(a * inner + row, STRIP), STRIP), :].astype(jnp.float32)

        signals = (
            [take(v_ref, a) for a in range(half)],
            [take(g_ref, a) * take(o_ref, a) for a in range(half)],
            [take(f_ref, a) for a in range(half)],
        )
        for which, blocks in enumerate(signals):
            cols = pl.ds(which * width, width)
            for freq, (re, im) in enumerate(real_dft(blocks + [None] * half)):
                split_store(ahi, alo, (freq, pl.ds(row, STRIP), cols), re)
                im = jnp.zeros_like(re) if im is None else im
                split_store(ahi, alo, (freq, pl.ds(pl.multiple_of(inner + row, STRIP), STRIP), cols), im)
        return 0

    @pl.when(k == 0)
    def _():
        lax.fori_loop(0, inner // STRIP, spread, 0)

    spec = dot3(fh[0], fl[0], ahi[k], alo[k])
    vr, gr, fr = (spec[:inner, i * width:(i + 1) * width] for i in range(3))
    vi, gi, fi = (spec[inner:, i * width:(i + 1) * width] for i in range(3))
    for i, (re, im) in enumerate((
        (vr * fr - vi * fi, vr * fi + vi * fr),
        (gr * fr + gi * fi, gi * fr - gr * fi),
        (gr * vr + gi * vi, gi * vr - gr * vi),
    )):
        hi, lo = split(jnp.concatenate([re, im], 0))
        back[k, :, pl.ds(i * width, width)] = dot3(ih[0], il[0], hi, lo)

    skip = s_ref[...]

    def gather(strip, _):
        row = pl.multiple_of(strip * STRIP, STRIP)

        def blocks_of(which):
            cols = pl.ds(which * width, width)
            hs = []
            for freq in range(half + 1):
                re = back[freq, pl.ds(row, STRIP), cols]
                if freq in (0, half):
                    hs.append((re, None))
                else:
                    hs.append((re, back[freq, pl.ds(pl.multiple_of(inner + row, STRIP), STRIP), cols]))
            return real_inverse(hs)

        def rows(a):
            return pl.ds(pl.multiple_of(a * inner + row, STRIP), STRIP)

        for a, conv in enumerate(blocks_of(0)):
            gate = g_ref[rows(a), :].astype(jnp.float32)
            grad = o_ref[rows(a), :].astype(jnp.float32)
            mixer = conv + skip * v_ref[rows(a), :].astype(jnp.float32)
            mixed_ref[rows(a), :] = (gate * mixer).astype(jnp.bfloat16)
            ggate_ref[rows(a), :] = (grad * mixer).astype(jnp.bfloat16)
        for a, conv in enumerate(blocks_of(1)):
            gm = g_ref[rows(a), :].astype(jnp.float32) * o_ref[rows(a), :].astype(jnp.float32)
            gval_ref[rows(a), :] = (conv + skip * gm).astype(jnp.bfloat16)
        for a, conv in enumerate(blocks_of(2)):
            gfil_ref[rows(a), :] = conv
        return 0

    @pl.when(k == half)
    def _():
        lax.fori_loop(0, inner // STRIP, gather, 0)


def local_mix(values, gates, grads, filters, skips):
    length, width = values.shape
    outer, inner = plan(length)
    pad = -width % LANES
    if pad:
        values, gates, grads, filters, skips = (
            jnp.pad(x, ((0, 0), (0, pad))) for x in (values, gates, grads, filters, skips)
        )
    full = width + pad
    half = outer // 2
    shape = (length, full)
    vmem = pl.BlockSpec(memory_space=pltpu.VMEM)
    table = pl.BlockSpec((1, 2 * inner, 2 * inner), lambda k: (k, 0, 0))
    outs = pl.pallas_call(
        partial(local_kernel, outer, inner),
        out_shape=[jax.ShapeDtypeStruct(shape, t) for t in (jnp.bfloat16,) * 3 + (jnp.float32,)],
        grid=(half + 1,),
        in_specs=[vmem] * 5 + [table] * 4,
        out_specs=[vmem] * 4,
        scratch_shapes=[
            pltpu.VMEM((half + 1, 2 * inner, 3 * full), jnp.bfloat16),
            pltpu.VMEM((half + 1, 2 * inner, 3 * full), jnp.bfloat16),
            pltpu.VMEM((half + 1, 2 * inner, 3 * full), jnp.float32),
        ],
        compiler_params=pltpu.CompilerParams(vmem_limit_bytes=(58 if pad else 40) * 2**20),
    )(values, gates, grads, filters, skips, *(jnp.asarray(t) for t in tables(length)))
    return [x[:, :width] for x in outs] if pad else outs


def on_device(values, gates, filters, skips, grad_out):
    rows, columns = values.shape
    group = lax.axis_size("context")
    width = columns // group
    to_channels = partial(lax.all_to_all, axis_name="context", split_axis=1, concat_axis=0, tiled=True)
    to_rows = partial(lax.all_to_all, axis_name="context", split_axis=0, concat_axis=1, tiled=True)
    mine = lax.dynamic_slice_in_dim(skips, lax.axis_index("context") * width, width, 0)
    mixed, ggate, gval, gfil = local_mix(
        to_channels(values), to_channels(gates), to_channels(grad_out), to_channels(filters), mine[None, :]
    )
    return to_rows(mixed), to_rows(ggate), to_rows(gval), to_rows(lax.psum(gfil, "dp"))


def solution(mesh):
    placed = (P("context", "dp"), P("context", "dp"), P("context", None), P("dp"), P("context", "dp"))
    return jax.shard_map(
        on_device,
        mesh=mesh,
        in_specs=placed,
        out_specs=(P("context", "dp"), P("context", "dp"), P("context", "dp"), P("context", None)),
        check_vma=False,
    )
```

```python
from functools import partial
import math

import jax
import jax.numpy as jnp
import numpy as np
from jax import lax
from jax.experimental import pallas as pl
from jax.experimental.pallas import tpu as pltpu
from jax.sharding import PartitionSpec as P

LANES = 128
STRIP = 16
MESH = pl.DeviceIdType.MESH


def plan(length):
    inner = 128
    while 2 * length // inner > 32:
        inner *= 2
    return 2 * length // inner, inner


def tables(length):
    outer, inner = plan(length)
    total = 2 * length
    pos = np.arange(inner, dtype=np.int64)[None, :]
    freq = np.arange(inner, dtype=np.int64)[:, None]
    fwd, inv = [], []
    for k in range(outer // 2 + 1):
        angle = -2.0 * np.pi / total * ((pos * (k + outer * freq)) % total)
        c, s = np.cos(angle), np.sin(angle)
        m = np.block([[c, -s], [s, c]])
        fwd.append(m)
        weight = (1.0 if k in (0, outer // 2) else 1.0) / total / math.sqrt(length)
        inv.append(m.T * weight)

    def split(stack):
        full = np.stack(stack).astype(np.float32)
        hi = full.astype(jnp.bfloat16)
        lo = (full - hi.astype(np.float32)).astype(jnp.bfloat16)
        return hi, lo

    return split(fwd) + split(inv)


def add(a, b):
    if a is None:
        return b
    return a if b is None else a + b


def sub(a, b):
    if b is None:
        return a
    return -b if a is None else a - b


def rotate(z, turn):
    re, im = z
    eighth = round(turn * 8) % 8 if abs(turn * 8 - round(turn * 8)) < 1e-9 else None
    if eighth == 0:
        return z
    if eighth == 4:
        return sub(None, re) if re is not None else None, sub(None, im) if im is not None else None
    if eighth == 2:
        return (None if im is None else -im), re
    if eighth == 6:
        return im, (None if re is None else -re)
    c, s = math.cos(2 * math.pi * turn), math.sin(2 * math.pi * turn)
    if im is None:
        return (None, None) if re is None else (re * c, re * s)
    if re is None:
        return im * -s, im * c
    if eighth is not None:
        if eighth == 1:
            return (re - im) * c, (re + im) * c
        if eighth == 3:
            return (re + im) * c, (im - re) * -c
        if eighth == 5:
            return (re - im) * c, (re + im) * c
        return (re + im) * c, (im - re) * c
    return re * c - im * s, re * s + im * c


def real_dft(xs):
    n = len(xs)
    if n == 1:
        return [(xs[0], None)]
    even, odd = real_dft(xs[::2]), real_dft(xs[1::2])
    out = [None] * (n // 2 + 1)
    for k in range(n // 4 + 1):
        er, ei = even[k]
        rr, ri = rotate(odd[k], -k / n)
        out[k] = (add(er, rr), add(ei, ri))
        if n // 2 - k != k:
            dr, di = sub(er, rr), sub(ei, ri)
            out[n // 2 - k] = (dr, None if di is None else -di)
    return out


def real_inverse(hs):
    n = 2 * (len(hs) - 1)
    if n == 2:
        return [add(hs[0][0], hs[1][0])]
    even, odd = [], []
    for k in range(n // 4 + 1):
        ar, ai = hs[k]
        br, bi = hs[n // 2 - k]
        if k == n // 4:
            even.append((ar + ar, None))
            odd.append((-(ai + ai), None))
            continue
        even.append((add(ar, br), sub(ai, bi)))
        odd.append(rotate((sub(ar, br), add(ai, bi)), k / n))
    out = [None] * (n // 2)
    out[::2] = real_inverse(even)
    out[1::2] = real_inverse(odd)
    return out


def split_store(hi_ref, lo_ref, index, value):
    hi = value.astype(jnp.bfloat16)
    hi_ref[index] = hi
    lo_ref[index] = (value - hi.astype(jnp.float32)).astype(jnp.bfloat16)


def split(value):
    hi = value.astype(jnp.bfloat16)
    return hi, (value - hi.astype(jnp.float32)).astype(jnp.bfloat16)


def dot3(mat_hi, mat_lo, hi, lo):
    dot = partial(jnp.dot, preferred_element_type=jnp.float32)
    return dot(mat_hi, hi) + dot(mat_hi, lo) + dot(mat_lo, hi)


def local_kernel(outer, inner, v_ref, g_ref, o_ref, f_ref, s_ref, fh, fl, ih, il,
                 mixed_ref, ggate_ref, gval_ref, gfil_ref, ahi, alo, back):
    half = outer // 2
    width = v_ref.shape[1]
    k = pl.program_id(0)

    def spread(strip, _):
        row = pl.multiple_of(strip * STRIP, STRIP)

        def take(ref, a):
            return ref[pl.ds(pl.multiple_of(a * inner + row, STRIP), STRIP), :].astype(jnp.float32)

        signals = (
            [take(v_ref, a) for a in range(half)],
            [take(g_ref, a) * take(o_ref, a) for a in range(half)],
            [take(f_ref, a) for a in range(half)],
        )
        for which, blocks in enumerate(signals):
            cols = pl.ds(which * width, width)
            for freq, (re, im) in enumerate(real_dft(blocks + [None] * half)):
                split_store(ahi, alo, (freq, pl.ds(row, STRIP), cols), re)
                im = jnp.zeros_like(re) if im is None else im
                split_store(ahi, alo, (freq, pl.ds(pl.multiple_of(inner + row, STRIP), STRIP), cols), im)
        return 0

    @pl.when(k == 0)
    def _():
        lax.fori_loop(0, inner // STRIP, spread, 0)

    spec = dot3(fh[0], fl[0], ahi[k], alo[k])
    vr, gr, fr = (spec[:inner, i * width:(i + 1) * width] for i in range(3))
    vi, gi, fi = (spec[inner:, i * width:(i + 1) * width] for i in range(3))
    for i, (re, im) in enumerate((
        (vr * fr - vi * fi, vr * fi + vi * fr),
        (gr * fr + gi * fi, gi * fr - gr * fi),
        (gr * vr + gi * vi, gi * vr - gr * vi),
    )):
        hi, lo = split(jnp.concatenate([re, im], 0))
        back[k, :, pl.ds(i * width, width)] = dot3(ih[0], il[0], hi, lo)

    skip = s_ref[...]

    def gather(strip, _):
        row = pl.multiple_of(strip * STRIP, STRIP)

        def blocks_of(which):
            cols = pl.ds(which * width, width)
            hs = []
            for freq in range(half + 1):
                re = back[freq, pl.ds(row, STRIP), cols]
                if freq in (0, half):
                    hs.append((re, None))
                else:
                    hs.append((re, back[freq, pl.ds(pl.multiple_of(inner + row, STRIP), STRIP), cols]))
            return real_inverse(hs)

        def rows(a):
            return pl.ds(pl.multiple_of(a * inner + row, STRIP), STRIP)

        for a, conv in enumerate(blocks_of(0)):
            gate = g_ref[rows(a), :].astype(jnp.float32)
            grad = o_ref[rows(a), :].astype(jnp.float32)
            mixer = conv + skip * v_ref[rows(a), :].astype(jnp.float32)
            mixed_ref[rows(a), :] = (gate * mixer).astype(jnp.bfloat16)
            ggate_ref[rows(a), :] = (grad * mixer).astype(jnp.bfloat16)
        for a, conv in enumerate(blocks_of(1)):
            gm = g_ref[rows(a), :].astype(jnp.float32) * o_ref[rows(a), :].astype(jnp.float32)
            gval_ref[rows(a), :] = (conv + skip * gm).astype(jnp.bfloat16)
        for a, conv in enumerate(blocks_of(2)):
            gfil_ref[rows(a), :] = conv
        return 0

    @pl.when(k == half)
    def _():
        lax.fori_loop(0, inner // STRIP, gather, 0)


def local_mix(values, gates, grads, filters, skips):
    length, width = values.shape
    outer, inner = plan(length)
    pad = -width % LANES
    if pad:
        values, gates, grads, filters, skips = (
            jnp.pad(x, ((0, 0), (0, pad))) for x in (values, gates, grads, filters, skips)
        )
    full = width + pad
    half = outer // 2
    shape = (length, full)
    vmem = pl.BlockSpec(memory_space=pltpu.VMEM)
    table = pl.BlockSpec((1, 2 * inner, 2 * inner), lambda k: (k, 0, 0))
    outs = pl.pallas_call(
        partial(local_kernel, outer, inner),
        out_shape=[jax.ShapeDtypeStruct(shape, t) for t in (jnp.bfloat16,) * 3 + (jnp.float32,)],
        grid=(half + 1,),
        in_specs=[vmem] * 5 + [table] * 4,
        out_specs=[vmem] * 4,
        scratch_shapes=[
            pltpu.VMEM((half + 1, 2 * inner, 3 * full), jnp.bfloat16),
            pltpu.VMEM((half + 1, 2 * inner, 3 * full), jnp.bfloat16),
            pltpu.VMEM((half + 1, 2 * inner, 3 * full), jnp.float32),
        ],
        compiler_params=pltpu.CompilerParams(vmem_limit_bytes=(58 if pad else 40) * 2**20),
    )(values, gates, grads, filters, skips, *(jnp.asarray(t) for t in tables(length)))
    return [x[:, :width] for x in outs] if pad else outs


def fused_kernel(outer, inner, n_dp, n_ctx, v_in, g_in, o_in, f_in, s_ref, fh_in, fl_in, ih_in, il_in,
                 mixed_out, ggate_out, gval_out, gfil_out,
                 v_ref, g_ref, o_ref, f_ref, fh, fl, ih, il, ahi, alo, spec, back,
                 mixed_ref, ggate_ref, gval_ref, gfil_ref, rs_buf, piece,
                 tab_sem, own_sem, in_send, in_recv, out_send, out_recv,
                 rs_send, rs_recv, pc_send, pc_recv, bc_send, bc_recv):
    half = outer // 2
    length, width = v_ref.shape
    rows_here = length // n_ctx
    rows_piece = length // n_dp
    dp, ctx = lax.axis_index("dp"), lax.axis_index("context")
    f32 = jnp.float32
    dot = partial(jnp.dot, preferred_element_type=f32)

    def ctx_at(step):
        return lax.rem(ctx + step + n_ctx, n_ctx)

    def dp_at(step):
        return lax.rem(dp + step + n_dp, n_dp)

    def block_rows(p):
        return pl.ds(pl.multiple_of(p * rows_here, 16), rows_here)

    def block_cols(p):
        return pl.ds(pl.multiple_of(p * width, LANES), width)

    loads = [
        pltpu.make_async_copy(src, dst, tab_sem.at[i])
        for i, (src, dst) in enumerate(((fh_in, fh), (fl_in, fl), (ih_in, ih), (il_in, il)))
    ]
    arrays = ((v_in, v_ref), (g_in, g_ref), (o_in, o_ref), (f_in, f_ref))
    own = [
        pltpu.make_async_copy(src.at[:, block_cols(ctx)], dst.at[block_rows(ctx), :], own_sem.at[i])
        for i, (src, dst) in enumerate(arrays)
    ]
    for copy in own + loads:
        copy.start()

    barrier = pltpu.get_barrier_semaphore()
    for step in range(1, n_ctx):
        pl.semaphore_signal(barrier, inc=1, device_id={"context": ctx_at(step)}, device_id_type=MESH)
    for step in range(1, n_dp):
        pl.semaphore_signal(barrier, inc=1, device_id={"dp": dp_at(step)}, device_id_type=MESH)
    pl.semaphore_wait(barrier, n_ctx - 1 + n_dp - 1)

    def inbound(i, step):
        src, dst = arrays[i]
        return pltpu.make_async_remote_copy(
            src_ref=src.at[:, block_cols(ctx_at(step))],
            dst_ref=dst.at[block_rows(ctx_at(-step)), :],
            send_sem=in_send.at[i, step],
            recv_sem=in_recv.at[i, step],
            device_id={"context": ctx_at(step)},
            device_id_type=MESH,
        )

    def outbound_in(i, step):
        src, dst = arrays[i]
        return pltpu.make_async_remote_copy(
            src_ref=src.at[:, block_cols(ctx_at(step))],
            dst_ref=dst.at[block_rows(ctx), :],
            send_sem=in_send.at[i, step],
            recv_sem=in_recv.at[i, step],
            device_id={"context": ctx_at(step)},
            device_id_type=MESH,
        )

    for i in range(4):
        for step in range(1, n_ctx):
            outbound_in(i, step).start()

    def arrived(i):
        own[i].wait()
        for step in range(1, n_ctx):
            inbound(i, step).wait_recv()

    def take(ref, a, row):
        return ref[pl.ds(pl.multiple_of(a * inner + row, STRIP), STRIP), :].astype(f32)

    def spread(which, blocks, row):
        cols = pl.ds(which * width, width)
        for freq, (re, im) in enumerate(real_dft(blocks + [None] * half)):
            split_store(ahi, alo, (freq, pl.ds(row, STRIP), cols), re)
            im = jnp.zeros_like(re) if im is None else im
            split_store(ahi, alo, (freq, pl.ds(pl.multiple_of(inner + row, STRIP), STRIP), cols), im)

    def gather(which, row):
        cols = pl.ds(which * width, width)
        hs = []
        for freq in range(half + 1):
            re = back[freq, pl.ds(row, STRIP), cols]
            if freq in (0, half):
                hs.append((re, None))
            else:
                hs.append((re, back[freq, pl.ds(pl.multiple_of(inner + row, STRIP), STRIP), cols]))
        return real_inverse(hs)

    def strips(body):
        def run(strip, carry):
            body(pl.multiple_of(strip * STRIP, STRIP))
            return carry

        lax.fori_loop(0, inner // STRIP, run, 0)

    def invert(k, which, re, im):
        hi, lo = split(jnp.concatenate([re, im], 0))
        back[k, :, pl.ds(which * width, width)] = dot3(ih[k], il[k], hi, lo)

    arrived(0)

    def spread_values(row):
        spread(0, [take(v_ref, a, row) for a in range(half)], row)

    strips(spread_values)
    arrived(1)
    arrived(2)

    def spread_grads(row):
        spread(1, [take(g_ref, a, row) * take(o_ref, a, row) for a in range(half)], row)

    strips(spread_grads)
    for copy in loads:
        copy.wait()

    def first(k, carry):
        both = dot3(fh[k], fl[k], ahi[k, :, : 2 * width], alo[k, :, : 2 * width])
        spec[k] = both
        vr, gr = both[:inner, :width], both[:inner, width:]
        vi, gi = both[inner:, :width], both[inner:, width:]
        invert(k, 2, gr * vr + gi * vi, gi * vr - gr * vi)
        return carry

    lax.fori_loop(0, half + 1, first, 0)

    def gather_filters(row):
        for a, conv in enumerate(gather(2, row)):
            gfil_ref[pl.ds(pl.multiple_of(a * inner + row, STRIP), STRIP), :] = conv

    strips(gather_filters)

    def piece_rows(d):
        place = lax.rem(d, n_ctx) * (n_dp // n_ctx) + d // n_ctx
        return pl.ds(pl.multiple_of(place * rows_piece, 8), rows_piece)

    scatter = [
        pltpu.make_async_remote_copy(
            src_ref=gfil_ref.at[piece_rows(dp_at(step)), :],
            dst_ref=rs_buf.at[step],
            send_sem=rs_send.at[step],
            recv_sem=rs_recv.at[step],
            device_id={"dp": dp_at(step)},
            device_id_type=MESH,
        )
        for step in range(1, n_dp)
    ]
    for copy in scatter:
        copy.start()

    arrived(3)

    def spread_filters(row):
        spread(2, [take(f_ref, a, row) for a in range(half)], row)

    strips(spread_filters)

    def second(k, carry):
        filt = dot3(fh[k], fl[k], ahi[k, :, 2 * width:], alo[k, :, 2 * width:])
        fr, fi = filt[:inner], filt[inner:]
        both = spec[k]
        vr, gr = both[:inner, :width], both[:inner, width:]
        vi, gi = both[inner:, :width], both[inner:, width:]
        invert(k, 0, vr * fr - vi * fi, vr * fi + vi * fr)
        invert(k, 1, gr * fr + gi * fi, gi * fr - gr * fi)
        return carry

    lax.fori_loop(0, half + 1, second, 0)
    skip = s_ref[...]

    def finish(row):
        def rows(a):
            return pl.ds(pl.multiple_of(a * inner + row, STRIP), STRIP)

        for a, conv in enumerate(gather(0, row)):
            gate, grad = take(g_ref, a, row), take(o_ref, a, row)
            mixer = conv + skip * take(v_ref, a, row)
            mixed_ref[rows(a), :] = (gate * mixer).astype(jnp.bfloat16)
            ggate_ref[rows(a), :] = (grad * mixer).astype(jnp.bfloat16)
        for a, conv in enumerate(gather(1, row)):
            gm = take(g_ref, a, row) * take(o_ref, a, row)
            gval_ref[rows(a), :] = (conv + skip * gm).astype(jnp.bfloat16)

    strips(finish)

    results = ((mixed_ref, mixed_out), (ggate_ref, ggate_out), (gval_ref, gval_out))

    def returned(i, step, landing):
        src, dst = results[i]
        return pltpu.make_async_remote_copy(
            src_ref=src.at[block_rows(ctx_at(step)), :],
            dst_ref=dst.at[:, block_cols(landing)],
            send_sem=out_send.at[i, step],
            recv_sem=out_recv.at[i, step],
            device_id={"context": ctx_at(step)},
            device_id_type=MESH,
        )

    for i in range(3):
        for step in range(1, n_ctx):
            returned(i, step, ctx).start()
    kept = [
        pltpu.make_async_copy(src.at[block_rows(ctx), :], dst.at[:, block_cols(ctx)], own_sem.at[i])
        for i, (src, dst) in enumerate(results)
    ]
    for copy in kept:
        copy.start()

    total = gfil_ref[piece_rows(dp), :]
    for step, copy in zip(range(1, n_dp), scatter):
        copy.wait_recv()
        total = total + rs_buf[step]
    piece[:, block_cols(ctx)] = total

    holder = lax.rem(dp, n_ctx)
    part = dp // n_ctx
    gap = lax.rem(ctx - holder + n_ctx, n_ctx)

    def part_rows(j):
        return pl.ds(pl.multiple_of(j * rows_piece, 8), rows_piece)

    def collect(which, c):
        return pltpu.make_async_remote_copy(
            src_ref=piece.at[:, block_cols(c)],
            dst_ref=piece.at[:, block_cols(c)],
            send_sem=pc_send.at[which],
            recv_sem=pc_recv.at[which],
            device_id={"context": holder},
            device_id_type=MESH,
        )

    def cast(step, j):
        return pltpu.make_async_remote_copy(
            src_ref=piece,
            dst_ref=gfil_out.at[part_rows(j), :],
            send_sem=bc_send.at[step],
            recv_sem=bc_recv.at[j],
            device_id={"dp": dp_at(step)},
            device_id_type=MESH,
        )

    @pl.when(ctx != holder)
    def _():
        copy = collect(gap, ctx)
        copy.start()
        copy.wait_send()

    @pl.when(ctx == holder)
    def _():
        for step in range(1, n_ctx):
            collect(step, ctx_at(step)).wait_recv()
        for step in range(1, n_dp):
            cast(step, part).start()
        mine = pltpu.make_async_copy(piece, gfil_out.at[part_rows(part), :], own_sem.at[3])
        mine.start()
        mine.wait()
        for step in range(1, n_dp):
            cast(step, part).wait_send()

    for j in range(n_dp // n_ctx):
        @pl.when(dp != ctx + j * n_ctx)
        def _():
            cast(1, j).wait_recv()

    for copy in kept:
        copy.wait()
    for i in range(3):
        for step in range(1, n_ctx):
            returned(i, step, ctx_at(-step)).wait_recv()
            returned(i, step, ctx).wait_send()
    for i in range(4):
        for step in range(1, n_ctx):
            outbound_in(i, step).wait_send()
    for copy in scatter:
        copy.wait_send()


def fused(values, gates, grads, filters, skips, n_dp, n_ctx):
    rows, columns = values.shape
    length, width = rows * n_ctx, columns // n_ctx
    outer, inner = plan(length)
    half = outer // 2
    vmem = pl.BlockSpec(memory_space=pltpu.VMEM)
    anywhere = pl.BlockSpec(memory_space=pl.ANY)
    bf16, f32 = jnp.bfloat16, jnp.float32
    full = (length, width)
    mats = (half + 1, 2 * inner, 2 * inner)
    rows_piece = length // n_dp
    dma = pltpu.SemaphoreType.DMA
    return pl.pallas_call(
        partial(fused_kernel, outer, inner, n_dp, n_ctx),
        out_shape=[jax.ShapeDtypeStruct((rows, columns), t) for t in (bf16, bf16, bf16, f32)],
        in_specs=[anywhere] * 4 + [vmem] + [anywhere] * 4,
        out_specs=[anywhere] * 4,
        scratch_shapes=[pltpu.VMEM(full, t) for t in (bf16, bf16, bf16, f32)]
        + [pltpu.VMEM(mats, bf16)] * 4
        + [
            pltpu.VMEM((half + 1, 2 * inner, 3 * width), bf16),
            pltpu.VMEM((half + 1, 2 * inner, 3 * width), bf16),
            pltpu.VMEM((half + 1, 2 * inner, 2 * width), f32),
            pltpu.VMEM((half + 1, 2 * inner, 3 * width), f32),
        ]
        + [pltpu.VMEM(full, t) for t in (bf16, bf16, bf16, f32)]
        + [
            pltpu.VMEM((n_dp, rows_piece, width), f32),
            pltpu.VMEM((rows_piece, columns), f32),
            dma((4,)), dma((4,)), dma((4, n_ctx)), dma((4, n_ctx)), dma((3, n_ctx)), dma((3, n_ctx)),
            dma((n_dp,)), dma((n_dp,)), dma((n_ctx,)), dma((n_ctx,)), dma((n_dp,)), dma((n_dp // n_ctx,)),
        ],
        compiler_params=pltpu.CompilerParams(
            collective_id=0, has_side_effects=True, vmem_limit_bytes=48 * 2**20
        ),
    )(values, gates, grads, filters, skips, *(jnp.asarray(t) for t in tables(length)))


def on_device(values, gates, filters, skips, grad_out):
    rows, columns = values.shape
    group = lax.axis_size("context")
    width = columns // group
    to_channels = partial(lax.all_to_all, axis_name="context", split_axis=1, concat_axis=0, tiled=True)
    to_rows = partial(lax.all_to_all, axis_name="context", split_axis=0, concat_axis=1, tiled=True)
    mine = lax.dynamic_slice_in_dim(skips, lax.axis_index("context") * width, width, 0)
    n_dp = lax.axis_size("dp")
    if width % LANES == 0 and n_dp % group == 0:
        return tuple(fused(values, gates, grad_out, filters, mine[None, :], n_dp, group))
    mixed, ggate, gval, gfil = local_mix(
        to_channels(values), to_channels(gates), to_channels(grad_out), to_channels(filters), mine[None, :]
    )
    return to_rows(mixed), to_rows(ggate), to_rows(gval), to_rows(lax.psum(gfil, "dp"))


def solution(mesh):
    placed = (P("context", "dp"), P("context", "dp"), P("context", None), P("dp"), P("context", "dp"))
    return jax.shard_map(
        on_device,
        mesh=mesh,
        in_specs=placed,
        out_specs=(P("context", "dp"), P("context", "dp"), P("context", "dp"), P("context", None)),
        check_vma=False,
    )
```

```python
from functools import partial
import math

import jax
import jax.numpy as jnp
import numpy as np
from jax import lax
from jax.experimental import pallas as pl
from jax.experimental.pallas import tpu as pltpu
from jax.sharding import PartitionSpec as P

LANES = 128
STRIP = 16
MESH = pl.DeviceIdType.MESH


def plan(length):
    inner = 128
    while 2 * length // inner > 32:
        inner *= 2
    return 2 * length // inner, inner


def tables(length):
    outer, inner = plan(length)
    total = 2 * length
    pos = np.arange(inner, dtype=np.int64)[None, :]
    freq = np.arange(inner, dtype=np.int64)[:, None]
    fwd, inv = [], []
    for k in range(outer // 2 + 1):
        angle = -2.0 * np.pi / total * ((pos * (k + outer * freq)) % total)
        c, s = np.cos(angle), np.sin(angle)
        m = np.block([[c, -s], [s, c]])
        fwd.append(m)
        weight = (1.0 if k in (0, outer // 2) else 1.0) / total / math.sqrt(length)
        inv.append(m.T * weight)

    def split(stack):
        full = np.stack(stack).astype(np.float32)
        hi = full.astype(jnp.bfloat16)
        lo = (full - hi.astype(np.float32)).astype(jnp.bfloat16)
        return hi, lo

    return split(fwd) + split(inv)


def add(a, b):
    if a is None:
        return b
    return a if b is None else a + b


def sub(a, b):
    if b is None:
        return a
    return -b if a is None else a - b


def rotate(z, turn):
    re, im = z
    eighth = round(turn * 8) % 8 if abs(turn * 8 - round(turn * 8)) < 1e-9 else None
    if eighth == 0:
        return z
    if eighth == 4:
        return sub(None, re) if re is not None else None, sub(None, im) if im is not None else None
    if eighth == 2:
        return (None if im is None else -im), re
    if eighth == 6:
        return im, (None if re is None else -re)
    c, s = math.cos(2 * math.pi * turn), math.sin(2 * math.pi * turn)
    if im is None:
        return (None, None) if re is None else (re * c, re * s)
    if re is None:
        return im * -s, im * c
    if eighth is not None:
        if eighth == 1:
            return (re - im) * c, (re + im) * c
        if eighth == 3:
            return (re + im) * c, (im - re) * -c
        if eighth == 5:
            return (re - im) * c, (re + im) * c
        return (re + im) * c, (im - re) * c
    return re * c - im * s, re * s + im * c


def real_dft(xs):
    n = len(xs)
    if n == 1:
        return [(xs[0], None)]
    even, odd = real_dft(xs[::2]), real_dft(xs[1::2])
    out = [None] * (n // 2 + 1)
    for k in range(n // 4 + 1):
        er, ei = even[k]
        rr, ri = rotate(odd[k], -k / n)
        out[k] = (add(er, rr), add(ei, ri))
        if n // 2 - k != k:
            dr, di = sub(er, rr), sub(ei, ri)
            out[n // 2 - k] = (dr, None if di is None else -di)
    return out


def real_inverse(hs):
    n = 2 * (len(hs) - 1)
    if n == 2:
        return [add(hs[0][0], hs[1][0])]
    even, odd = [], []
    for k in range(n // 4 + 1):
        ar, ai = hs[k]
        br, bi = hs[n // 2 - k]
        if k == n // 4:
            even.append((ar + ar, None))
            odd.append((-(ai + ai), None))
            continue
        even.append((add(ar, br), sub(ai, bi)))
        odd.append(rotate((sub(ar, br), add(ai, bi)), k / n))
    out = [None] * (n // 2)
    out[::2] = real_inverse(even)
    out[1::2] = real_inverse(odd)
    return out


def split_store(hi_ref, lo_ref, index, value):
    hi = value.astype(jnp.bfloat16)
    hi_ref[index] = hi
    lo_ref[index] = (value - hi.astype(jnp.float32)).astype(jnp.bfloat16)


def split(value):
    hi = value.astype(jnp.bfloat16)
    return hi, (value - hi.astype(jnp.float32)).astype(jnp.bfloat16)


def dot3(mat_hi, mat_lo, hi, lo):
    dot = partial(jnp.dot, preferred_element_type=jnp.float32)
    return dot(mat_hi, hi) + dot(mat_hi, lo) + dot(mat_lo, hi)


def local_kernel(outer, inner, v_ref, g_ref, o_ref, f_ref, s_ref, fh, fl, ih, il,
                 mixed_ref, ggate_ref, gval_ref, gfil_ref, ahi, alo, back):
    half = outer // 2
    width = v_ref.shape[1]
    k = pl.program_id(0)

    def spread(strip, _):
        row = pl.multiple_of(strip * STRIP, STRIP)

        def take(ref, a):
            return ref[pl.ds(pl.multiple_of(a * inner + row, STRIP), STRIP), :].astype(jnp.float32)

        signals = (
            [take(v_ref, a) for a in range(half)],
            [take(g_ref, a) * take(o_ref, a) for a in range(half)],
            [take(f_ref, a) for a in range(half)],
        )
        for which, blocks in enumerate(signals):
            cols = pl.ds(which * width, width)
            for freq, (re, im) in enumerate(real_dft(blocks + [None] * half)):
                split_store(ahi, alo, (freq, pl.ds(row, STRIP), cols), re)
                im = jnp.zeros_like(re) if im is None else im
                split_store(ahi, alo, (freq, pl.ds(pl.multiple_of(inner + row, STRIP), STRIP), cols), im)
        return 0

    @pl.when(k == 0)
    def _():
        lax.fori_loop(0, inner // STRIP, spread, 0)

    spec = dot3(fh[0], fl[0], ahi[k], alo[k])
    vr, gr, fr = (spec[:inner, i * width:(i + 1) * width] for i in range(3))
    vi, gi, fi = (spec[inner:, i * width:(i + 1) * width] for i in range(3))
    for i, (re, im) in enumerate((
        (vr * fr - vi * fi, vr * fi + vi * fr),
        (gr * fr + gi * fi, gi * fr - gr * fi),
        (gr * vr + gi * vi, gi * vr - gr * vi),
    )):
        hi, lo = split(jnp.concatenate([re, im], 0))
        back[k, :, pl.ds(i * width, width)] = dot3(ih[0], il[0], hi, lo)

    skip = s_ref[...]

    def gather(strip, _):
        row = pl.multiple_of(strip * STRIP, STRIP)

        def blocks_of(which):
            cols = pl.ds(which * width, width)
            hs = []
            for freq in range(half + 1):
                re = back[freq, pl.ds(row, STRIP), cols]
                if freq in (0, half):
                    hs.append((re, None))
                else:
                    hs.append((re, back[freq, pl.ds(pl.multiple_of(inner + row, STRIP), STRIP), cols]))
            return real_inverse(hs)

        def rows(a):
            return pl.ds(pl.multiple_of(a * inner + row, STRIP), STRIP)

        for a, conv in enumerate(blocks_of(0)):
            gate = g_ref[rows(a), :].astype(jnp.float32)
            grad = o_ref[rows(a), :].astype(jnp.float32)
            mixer = conv + skip * v_ref[rows(a), :].astype(jnp.float32)
            mixed_ref[rows(a), :] = (gate * mixer).astype(jnp.bfloat16)
            ggate_ref[rows(a), :] = (grad * mixer).astype(jnp.bfloat16)
        for a, conv in enumerate(blocks_of(1)):
            gm = g_ref[rows(a), :].astype(jnp.float32) * o_ref[rows(a), :].astype(jnp.float32)
            gval_ref[rows(a), :] = (conv + skip * gm).astype(jnp.bfloat16)
        for a, conv in enumerate(blocks_of(2)):
            gfil_ref[rows(a), :] = conv
        return 0

    @pl.when(k == half)
    def _():
        lax.fori_loop(0, inner // STRIP, gather, 0)


def local_mix(values, gates, grads, filters, skips):
    length, width = values.shape
    outer, inner = plan(length)
    pad = -width % LANES
    if pad:
        values, gates, grads, filters, skips = (
            jnp.pad(x, ((0, 0), (0, pad))) for x in (values, gates, grads, filters, skips)
        )
    full = width + pad
    half = outer // 2
    shape = (length, full)
    vmem = pl.BlockSpec(memory_space=pltpu.VMEM)
    table = pl.BlockSpec((1, 2 * inner, 2 * inner), lambda k: (k, 0, 0))
    outs = pl.pallas_call(
        partial(local_kernel, outer, inner),
        out_shape=[jax.ShapeDtypeStruct(shape, t) for t in (jnp.bfloat16,) * 3 + (jnp.float32,)],
        grid=(half + 1,),
        in_specs=[vmem] * 5 + [table] * 4,
        out_specs=[vmem] * 4,
        scratch_shapes=[
            pltpu.VMEM((half + 1, 2 * inner, 3 * full), jnp.bfloat16),
            pltpu.VMEM((half + 1, 2 * inner, 3 * full), jnp.bfloat16),
            pltpu.VMEM((half + 1, 2 * inner, 3 * full), jnp.float32),
        ],
        compiler_params=pltpu.CompilerParams(vmem_limit_bytes=(58 if pad else 40) * 2**20),
    )(values, gates, grads, filters, skips, *(jnp.asarray(t) for t in tables(length)))
    return [x[:, :width] for x in outs] if pad else outs


def fused_kernel(outer, inner, n_dp, n_ctx, v_in, g_in, o_in, f_in, s_ref, fh_in, fl_in, ih_in, il_in,
                 mixed_out, ggate_out, gval_out, gfil_out,
                 v_ref, g_ref, o_ref, f_ref, fh, fl, ih, il, ahi, alo, spec, back,
                 mixed_ref, ggate_ref, gval_ref, gfil_ref, x_buf, z_buf, sum_ref,
                 tab_sem, own_sem, in_send, in_recv, out_send, out_recv,
                 x_send, x_recv, z_send, z_recv, pc_send, pc_recv, ag_send, fw_send, ag_recv):
    half = outer // 2
    length, width = v_ref.shape
    rows_here = length // n_ctx
    rows_piece = length // n_dp
    dp, ctx = lax.axis_index("dp"), lax.axis_index("context")
    f32 = jnp.float32
    dot = partial(jnp.dot, preferred_element_type=f32)

    def ctx_at(step):
        return lax.rem(ctx + step + n_ctx, n_ctx)

    n_z = n_dp // 2
    z, x = dp // 2, lax.rem(dp, 2)
    across = 2 * z + 1 - x

    def z_at(step):
        return lax.rem(z + step + n_z, n_z)

    def block_rows(p):
        return pl.ds(pl.multiple_of(p * rows_here, 16), rows_here)

    def block_cols(p):
        return pl.ds(pl.multiple_of(p * width, LANES), width)

    loads = [
        pltpu.make_async_copy(src, dst, tab_sem.at[i])
        for i, (src, dst) in enumerate(((fh_in, fh), (fl_in, fl), (ih_in, ih), (il_in, il)))
    ]
    arrays = ((v_in, v_ref), (g_in, g_ref), (o_in, o_ref), (f_in, f_ref))
    own = [
        pltpu.make_async_copy(src.at[:, block_cols(ctx)], dst.at[block_rows(ctx), :], own_sem.at[i])
        for i, (src, dst) in enumerate(arrays)
    ]
    for copy in own + loads:
        copy.start()

    barrier = pltpu.get_barrier_semaphore()
    for step in range(1, n_ctx):
        pl.semaphore_signal(barrier, inc=1, device_id={"context": ctx_at(step)}, device_id_type=MESH)
    pl.semaphore_signal(barrier, inc=1, device_id={"dp": across}, device_id_type=MESH)
    for step in range(1, n_z):
        pl.semaphore_signal(barrier, inc=1, device_id={"dp": 2 * z_at(step) + x}, device_id_type=MESH)
    pl.semaphore_wait(barrier, n_ctx - 1 + 1 + n_z - 1)

    def inbound(i, step):
        src, dst = arrays[i]
        return pltpu.make_async_remote_copy(
            src_ref=src.at[:, block_cols(ctx_at(step))],
            dst_ref=dst.at[block_rows(ctx_at(-step)), :],
            send_sem=in_send.at[i, step],
            recv_sem=in_recv.at[i, step],
            device_id={"context": ctx_at(step)},
            device_id_type=MESH,
        )

    def outbound_in(i, step):
        src, dst = arrays[i]
        return pltpu.make_async_remote_copy(
            src_ref=src.at[:, block_cols(ctx_at(step))],
            dst_ref=dst.at[block_rows(ctx), :],
            send_sem=in_send.at[i, step],
            recv_sem=in_recv.at[i, step],
            device_id={"context": ctx_at(step)},
            device_id_type=MESH,
        )

    for i in range(3):
        for step in range(1, n_ctx):
            outbound_in(i, step).start()

    def arrived(i):
        own[i].wait()
        for step in range(1, n_ctx):
            inbound(i, step).wait_recv()

    def take(ref, a, row):
        return ref[pl.ds(pl.multiple_of(a * inner + row, STRIP), STRIP), :].astype(f32)

    def spread(which, blocks, row):
        cols = pl.ds(which * width, width)
        for freq, (re, im) in enumerate(real_dft(blocks + [None] * half)):
            split_store(ahi, alo, (freq, pl.ds(row, STRIP), cols), re)
            im = jnp.zeros_like(re) if im is None else im
            split_store(ahi, alo, (freq, pl.ds(pl.multiple_of(inner + row, STRIP), STRIP), cols), im)

    def gather(which, row):
        cols = pl.ds(which * width, width)
        hs = []
        for freq in range(half + 1):
            re = back[freq, pl.ds(row, STRIP), cols]
            if freq in (0, half):
                hs.append((re, None))
            else:
                hs.append((re, back[freq, pl.ds(pl.multiple_of(inner + row, STRIP), STRIP), cols]))
        return real_inverse(hs)

    def strips(body):
        def run(strip, carry):
            body(pl.multiple_of(strip * STRIP, STRIP))
            return carry

        lax.fori_loop(0, inner // STRIP, run, 0)

    def invert(k, which, re, im):
        hi, lo = split(jnp.concatenate([re, im], 0))
        back[k, :, pl.ds(which * width, width)] = dot3(ih[k], il[k], hi, lo)

    arrived(0)

    def spread_values(row):
        spread(0, [take(v_ref, a, row) for a in range(half)], row)

    strips(spread_values)
    arrived(1)
    arrived(2)
    for step in range(1, n_ctx):
        outbound_in(3, step).start()

    def spread_grads(row):
        spread(1, [take(g_ref, a, row) * take(o_ref, a, row) for a in range(half)], row)

    strips(spread_grads)
    for copy in loads:
        copy.wait()

    def first(k, carry):
        both = dot3(fh[k], fl[k], ahi[k, :, : 2 * width], alo[k, :, : 2 * width])
        spec[k] = both
        vr, gr = both[:inner, :width], both[:inner, width:]
        vi, gi = both[inner:, :width], both[inner:, width:]
        invert(k, 2, gr * vr + gi * vi, gi * vr - gr * vi)
        return carry

    lax.fori_loop(0, half + 1, first, 0)

    def gather_filters(row):
        for a, conv in enumerate(gather(2, row)):
            gfil_ref[pl.ds(pl.multiple_of(a * inner + row, STRIP), STRIP), :] = conv

    strips(gather_filters)

    def piece_rows(d):
        place = lax.rem(d, n_ctx) * (n_dp // n_ctx) + d // n_ctx
        return pl.ds(pl.multiple_of(place * rows_piece, 8), rows_piece)

    cross = {
        step: pltpu.make_async_remote_copy(
            src_ref=gfil_ref.at[piece_rows(2 * z_at(step) + 1 - x), :],
            dst_ref=x_buf.at[step],
            send_sem=x_send.at[step],
            recv_sem=x_recv.at[step],
            device_id={"dp": across},
            device_id_type=MESH,
        )
        for step in range(n_z)
    }
    order = sorted(range(1, n_z), key=lambda step: abs(step - n_z // 2)) + [0]
    for step in order:
        cross[step].start()
    along = {
        step: pltpu.make_async_remote_copy(
            src_ref=x_buf.at[step],
            dst_ref=z_buf.at[step],
            send_sem=z_send.at[step],
            recv_sem=z_recv.at[step],
            device_id={"dp": 2 * z_at(step) + x},
            device_id_type=MESH,
        )
        for step in range(1, n_z)
    }

    arrived(3)

    def spread_filters(row):
        spread(2, [take(f_ref, a, row) for a in range(half)], row)

    strips(spread_filters)

    def second(k, carry):
        filt = dot3(fh[k], fl[k], ahi[k, :, 2 * width:], alo[k, :, 2 * width:])
        fr, fi = filt[:inner], filt[inner:]
        both = spec[k]
        vr, gr = both[:inner, :width], both[:inner, width:]
        vi, gi = both[inner:, :width], both[inner:, width:]
        invert(k, 0, vr * fr - vi * fi, vr * fi + vi * fr)
        invert(k, 1, gr * fr + gi * fi, gi * fr - gr * fi)
        return carry

    middle = (half + 1) // 2
    lax.fori_loop(0, middle, second, 0)
    for step in order[:-1]:
        cross[step].wait_recv()
        x_buf[step] = x_buf[step] + gfil_ref[piece_rows(2 * z_at(step) + x), :]
        along[step].start()
    lax.fori_loop(middle, half + 1, second, 0)
    skip = s_ref[...]

    def finish(row):
        def rows(a):
            return pl.ds(pl.multiple_of(a * inner + row, STRIP), STRIP)

        for a, conv in enumerate(gather(0, row)):
            gate, grad = take(g_ref, a, row), take(o_ref, a, row)
            mixer = conv + skip * take(v_ref, a, row)
            mixed_ref[rows(a), :] = (gate * mixer).astype(jnp.bfloat16)
            ggate_ref[rows(a), :] = (grad * mixer).astype(jnp.bfloat16)
        for a, conv in enumerate(gather(1, row)):
            gm = take(g_ref, a, row) * take(o_ref, a, row)
            gval_ref[rows(a), :] = (conv + skip * gm).astype(jnp.bfloat16)

    strips(finish)

    cross[0].wait_recv()
    total = gfil_ref[piece_rows(dp), :] + x_buf[0]
    for step in range(1, n_z):
        along[step].wait_recv()
        total = total + z_buf[step]
    sum_ref[...] = total

    holder = lax.rem(dp, n_ctx)
    part = dp // n_ctx
    gap = lax.rem(ctx - holder + n_ctx, n_ctx)

    def part_of(j, c):
        return gfil_out.at[pl.ds(pl.multiple_of(j * rows_piece, 8), rows_piece), block_cols(c)]

    def collect(which, c):
        return pltpu.make_async_remote_copy(
            src_ref=sum_ref,
            dst_ref=part_of(part, c),
            send_sem=pc_send.at[which],
            recv_sem=pc_recv.at[which],
            device_id={"context": holder},
            device_id_type=MESH,
        )

    def relay(j, c, target, sem):
        return pltpu.make_async_remote_copy(
            src_ref=part_of(j, c),
            dst_ref=part_of(j, c),
            send_sem=sem,
            recv_sem=ag_recv.at[j, c],
            device_id={"dp": target},
            device_id_type=MESH,
        )

    def onward(step, c):
        return relay(part, c, 2 * z_at(step) + x, ag_send.at[step, c])

    def sideways(j, c):
        return relay(j, c, across, fw_send.at[j, c])

    @pl.when(ctx != holder)
    def _():
        collect(gap, ctx).start()

    results = ((mixed_ref, mixed_out), (ggate_ref, ggate_out), (gval_ref, gval_out))

    def returned(i, step, landing):
        src, dst = results[i]
        return pltpu.make_async_remote_copy(
            src_ref=src.at[block_rows(ctx_at(step)), :],
            dst_ref=dst.at[:, block_cols(landing)],
            send_sem=out_send.at[i, step],
            recv_sem=out_recv.at[i, step],
            device_id={"context": ctx_at(step)},
            device_id_type=MESH,
        )

    for i in range(3):
        for step in range(1, n_ctx):
            returned(i, step, ctx).start()
    kept = [
        pltpu.make_async_copy(src.at[block_rows(ctx), :], dst.at[:, block_cols(ctx)], own_sem.at[i])
        for i, (src, dst) in enumerate(results)
    ]
    for copy in kept:
        copy.start()

    @pl.when(ctx == holder)
    def _():
        mine = pltpu.make_async_copy(sum_ref, part_of(part, ctx), own_sem.at[3])
        mine.start()
        mine.wait()
        for gap_here in range(n_ctx):
            c = ctx_at(gap_here)
            if gap_here:
                collect(gap_here, c).wait_recv()
            for step in order[:-1]:
                onward(step, c).start()
            sideways(part, c).start()

    parts = n_dp // n_ctx
    relays = []
    for j in range(parts):
        source = ctx + j * n_ctx
        relays.append(jnp.logical_and(lax.rem(source, 2) == x, source != dp))

    for gap_here in range(n_ctx):
        for j in range(parts):
            c = lax.rem(ctx + gap_here, n_ctx)

            @pl.when(relays[j])
            def _():
                sideways(j, c).wait_recv()
                sideways(j, c).start()

    for j in range(parts):
        @pl.when(lax.rem(ctx + j * n_ctx, 2) != x)
        def _():
            for c in range(n_ctx):
                sideways(j, c).wait_recv()

        @pl.when(lax.rem(ctx + j * n_ctx, 2) == x)
        def _():
            for c in range(n_ctx):
                sideways(j, c).wait_send()

    @pl.when(ctx == holder)
    def _():
        for gap_here in range(n_ctx):
            for step in order[:-1]:
                onward(step, ctx_at(gap_here)).wait_send()

    @pl.when(ctx != holder)
    def _():
        collect(gap, ctx).wait_send()

    for copy in kept:
        copy.wait()
    for i in range(3):
        for step in range(1, n_ctx):
            returned(i, step, ctx_at(-step)).wait_recv()
            returned(i, step, ctx).wait_send()
    for i in range(4):
        for step in range(1, n_ctx):
            outbound_in(i, step).wait_send()
    for step in range(n_z):
        cross[step].wait_send()
    for step in range(1, n_z):
        along[step].wait_send()


def hand_over_kernel(*refs):
    count = len(refs) // 2
    for src, dst in zip(refs[:count], refs[count:]):
        dst[...] = src[...]


def hand_over(arrays):
    vmem = pl.BlockSpec(memory_space=pltpu.VMEM)
    return pl.pallas_call(
        hand_over_kernel,
        out_shape=[jax.ShapeDtypeStruct(x.shape, x.dtype) for x in arrays],
        in_specs=[vmem] * len(arrays),
        out_specs=[vmem] * len(arrays),
    )(*arrays)


def fused(values, gates, grads, filters, skips, n_dp, n_ctx):
    rows, columns = values.shape
    length, width = rows * n_ctx, columns // n_ctx
    outer, inner = plan(length)
    half = outer // 2
    vmem = pl.BlockSpec(memory_space=pltpu.VMEM)
    anywhere = pl.BlockSpec(memory_space=pl.ANY)
    bf16, f32 = jnp.bfloat16, jnp.float32
    full = (length, width)
    mats = (half + 1, 2 * inner, 2 * inner)
    rows_piece = length // n_dp
    dma = pltpu.SemaphoreType.DMA
    return pl.pallas_call(
        partial(fused_kernel, outer, inner, n_dp, n_ctx),
        out_shape=[jax.ShapeDtypeStruct((rows, columns), t) for t in (bf16, bf16, bf16, f32)],
        in_specs=[anywhere] * 4 + [vmem] + [anywhere] * 4,
        out_specs=[anywhere] * 4,
        scratch_shapes=[pltpu.VMEM(full, t) for t in (bf16, bf16, bf16, f32)]
        + [pltpu.VMEM(mats, bf16)] * 4
        + [
            pltpu.VMEM((half + 1, 2 * inner, 3 * width), bf16),
            pltpu.VMEM((half + 1, 2 * inner, 3 * width), bf16),
            pltpu.VMEM((half + 1, 2 * inner, 2 * width), f32),
            pltpu.VMEM((half + 1, 2 * inner, 3 * width), f32),
        ]
        + [pltpu.VMEM(full, t) for t in (bf16, bf16, bf16, f32)]
        + [
            pltpu.VMEM((n_dp // 2, rows_piece, width), f32),
            pltpu.VMEM((n_dp // 2, rows_piece, width), f32),
            pltpu.VMEM((rows_piece, width), f32),
            dma((4,)), dma((4,)), dma((4, n_ctx)), dma((4, n_ctx)), dma((3, n_ctx)), dma((3, n_ctx)),
            dma((n_dp // 2,)), dma((n_dp // 2,)), dma((n_dp // 2,)), dma((n_dp // 2,)),
            dma((n_ctx,)), dma((n_ctx,)),
            dma((n_dp // 2, n_ctx)), dma((n_dp // n_ctx, n_ctx)), dma((n_dp // n_ctx, n_ctx)),
        ],
        compiler_params=pltpu.CompilerParams(
            collective_id=0, has_side_effects=True, vmem_limit_bytes=60 * 2**20
        ),
    )(values, gates, grads, filters, skips, *(jnp.asarray(t) for t in tables(length)))


def on_device(values, gates, filters, skips, grad_out):
    rows, columns = values.shape
    group = lax.axis_size("context")
    width = columns // group
    to_channels = partial(lax.all_to_all, axis_name="context", split_axis=1, concat_axis=0, tiled=True)
    to_rows = partial(lax.all_to_all, axis_name="context", split_axis=0, concat_axis=1, tiled=True)
    mine = lax.dynamic_slice_in_dim(skips, lax.axis_index("context") * width, width, 0)
    n_dp = lax.axis_size("dp")
    if width % LANES == 0 and n_dp % group == 0 and n_dp % 2 == 0 and group % 2 == 0:
        return tuple(hand_over(fused(values, gates, grad_out, filters, mine[None, :], n_dp, group)))
    mixed, ggate, gval, gfil = local_mix(
        to_channels(values), to_channels(gates), to_channels(grad_out), to_channels(filters), mine[None, :]
    )
    return to_rows(mixed), to_rows(ggate), to_rows(gval), to_rows(lax.psum(gfil, "dp"))


def solution(mesh):
    placed = (P("context", "dp"), P("context", "dp"), P("context", None), P("dp"), P("context", "dp"))
    return jax.shard_map(
        on_device,
        mesh=mesh,
        in_specs=placed,
        out_specs=(P("context", "dp"), P("context", "dp"), P("context", "dp"), P("context", None)),
        check_vma=False,
    )
```

```python
from functools import partial
import math

import jax
import jax.numpy as jnp
import numpy as np
from jax import lax
from jax.experimental import pallas as pl
from jax.experimental.pallas import tpu as pltpu
from jax.sharding import PartitionSpec as P

LANES = 128
STRIP = 16
MESH = pl.DeviceIdType.MESH


def plan(length):
    inner = 128
    while 2 * length // inner > 32:
        inner *= 2
    return 2 * length // inner, inner


def tables(length):
    outer, inner = plan(length)
    total = 2 * length
    pos = np.arange(inner, dtype=np.int64)[None, :]
    freq = np.arange(inner, dtype=np.int64)[:, None]
    fwd, inv = [], []
    for k in range(outer // 2 + 1):
        angle = -2.0 * np.pi / total * ((pos * (k + outer * freq)) % total)
        c, s = np.cos(angle), np.sin(angle)
        m = np.block([[c, -s], [s, c]])
        fwd.append(m)
        weight = (1.0 if k in (0, outer // 2) else 1.0) / total / math.sqrt(length)
        inv.append(m.T * weight)

    def split(stack):
        full = np.stack(stack).astype(np.float32)
        hi = full.astype(jnp.bfloat16)
        lo = (full - hi.astype(np.float32)).astype(jnp.bfloat16)
        return hi, lo

    return split(fwd) + split(inv)


def add(a, b):
    if a is None:
        return b
    return a if b is None else a + b


def sub(a, b):
    if b is None:
        return a
    return -b if a is None else a - b


def rotate(z, turn):
    re, im = z
    eighth = round(turn * 8) % 8 if abs(turn * 8 - round(turn * 8)) < 1e-9 else None
    if eighth == 0:
        return z
    if eighth == 4:
        return sub(None, re) if re is not None else None, sub(None, im) if im is not None else None
    if eighth == 2:
        return (None if im is None else -im), re
    if eighth == 6:
        return im, (None if re is None else -re)
    c, s = math.cos(2 * math.pi * turn), math.sin(2 * math.pi * turn)
    if im is None:
        return (None, None) if re is None else (re * c, re * s)
    if re is None:
        return im * -s, im * c
    if eighth is not None:
        if eighth == 1:
            return (re - im) * c, (re + im) * c
        if eighth == 3:
            return (re + im) * c, (im - re) * -c
        if eighth == 5:
            return (re - im) * c, (re + im) * c
        return (re + im) * c, (im - re) * c
    return re * c - im * s, re * s + im * c


def real_dft(xs):
    n = len(xs)
    if n == 1:
        return [(xs[0], None)]
    even, odd = real_dft(xs[::2]), real_dft(xs[1::2])
    out = [None] * (n // 2 + 1)
    for k in range(n // 4 + 1):
        er, ei = even[k]
        rr, ri = rotate(odd[k], -k / n)
        out[k] = (add(er, rr), add(ei, ri))
        if n // 2 - k != k:
            dr, di = sub(er, rr), sub(ei, ri)
            out[n // 2 - k] = (dr, None if di is None else -di)
    return out


def real_inverse(hs):
    n = 2 * (len(hs) - 1)
    if n == 2:
        return [add(hs[0][0], hs[1][0])]
    even, odd = [], []
    for k in range(n // 4 + 1):
        ar, ai = hs[k]
        br, bi = hs[n // 2 - k]
        if k == n // 4:
            even.append((ar + ar, None))
            odd.append((-(ai + ai), None))
            continue
        even.append((add(ar, br), sub(ai, bi)))
        odd.append(rotate((sub(ar, br), add(ai, bi)), k / n))
    out = [None] * (n // 2)
    out[::2] = real_inverse(even)
    out[1::2] = real_inverse(odd)
    return out


def split_store(hi_ref, lo_ref, index, value):
    hi = value.astype(jnp.bfloat16)
    hi_ref[index] = hi
    lo_ref[index] = (value - hi.astype(jnp.float32)).astype(jnp.bfloat16)


def split(value):
    hi = value.astype(jnp.bfloat16)
    return hi, (value - hi.astype(jnp.float32)).astype(jnp.bfloat16)


def dot3(mat_hi, mat_lo, hi, lo):
    dot = partial(jnp.dot, preferred_element_type=jnp.float32)
    return dot(mat_hi, hi) + dot(mat_hi, lo) + dot(mat_lo, hi)


def local_kernel(outer, inner, v_ref, g_ref, o_ref, f_ref, s_ref, fh, fl, ih, il,
                 mixed_ref, ggate_ref, gval_ref, gfil_ref, ahi, alo, back):
    half = outer // 2
    width = v_ref.shape[1]
    k = pl.program_id(0)

    def spread(strip, _):
        row = pl.multiple_of(strip * STRIP, STRIP)

        def take(ref, a):
            return ref[pl.ds(pl.multiple_of(a * inner + row, STRIP), STRIP), :].astype(jnp.float32)

        signals = (
            [take(v_ref, a) for a in range(half)],
            [take(g_ref, a) * take(o_ref, a) for a in range(half)],
            [take(f_ref, a) for a in range(half)],
        )
        for which, blocks in enumerate(signals):
            cols = pl.ds(which * width, width)
            for freq, (re, im) in enumerate(real_dft(blocks + [None] * half)):
                split_store(ahi, alo, (freq, pl.ds(row, STRIP), cols), re)
                im = jnp.zeros_like(re) if im is None else im
                split_store(ahi, alo, (freq, pl.ds(pl.multiple_of(inner + row, STRIP), STRIP), cols), im)
        return 0

    @pl.when(k == 0)
    def _():
        lax.fori_loop(0, inner // STRIP, spread, 0)

    spec = dot3(fh[0], fl[0], ahi[k], alo[k])
    vr, gr, fr = (spec[:inner, i * width:(i + 1) * width] for i in range(3))
    vi, gi, fi = (spec[inner:, i * width:(i + 1) * width] for i in range(3))
    for i, (re, im) in enumerate((
        (vr * fr - vi * fi, vr * fi + vi * fr),
        (gr * fr + gi * fi, gi * fr - gr * fi),
        (gr * vr + gi * vi, gi * vr - gr * vi),
    )):
        hi, lo = split(jnp.concatenate([re, im], 0))
        back[k, :, pl.ds(i * width, width)] = dot3(ih[0], il[0], hi, lo)

    skip = s_ref[...]

    def gather(strip, _):
        row = pl.multiple_of(strip * STRIP, STRIP)

        def blocks_of(which):
            cols = pl.ds(which * width, width)
            hs = []
            for freq in range(half + 1):
                re = back[freq, pl.ds(row, STRIP), cols]
                if freq in (0, half):
                    hs.append((re, None))
                else:
                    hs.append((re, back[freq, pl.ds(pl.multiple_of(inner + row, STRIP), STRIP), cols]))
            return real_inverse(hs)

        def rows(a):
            return pl.ds(pl.multiple_of(a * inner + row, STRIP), STRIP)

        for a, conv in enumerate(blocks_of(0)):
            gate = g_ref[rows(a), :].astype(jnp.float32)
            grad = o_ref[rows(a), :].astype(jnp.float32)
            mixer = conv + skip * v_ref[rows(a), :].astype(jnp.float32)
            mixed_ref[rows(a), :] = (gate * mixer).astype(jnp.bfloat16)
            ggate_ref[rows(a), :] = (grad * mixer).astype(jnp.bfloat16)
        for a, conv in enumerate(blocks_of(1)):
            gm = g_ref[rows(a), :].astype(jnp.float32) * o_ref[rows(a), :].astype(jnp.float32)
            gval_ref[rows(a), :] = (conv + skip * gm).astype(jnp.bfloat16)
        for a, conv in enumerate(blocks_of(2)):
            gfil_ref[rows(a), :] = conv
        return 0

    @pl.when(k == half)
    def _():
        lax.fori_loop(0, inner // STRIP, gather, 0)


def local_mix(values, gates, grads, filters, skips):
    length, width = values.shape
    outer, inner = plan(length)
    pad = -width % LANES
    if pad:
        values, gates, grads, filters, skips = (
            jnp.pad(x, ((0, 0), (0, pad))) for x in (values, gates, grads, filters, skips)
        )
    full = width + pad
    half = outer // 2
    shape = (length, full)
    vmem = pl.BlockSpec(memory_space=pltpu.VMEM)
    table = pl.BlockSpec((1, 2 * inner, 2 * inner), lambda k: (k, 0, 0))
    outs = pl.pallas_call(
        partial(local_kernel, outer, inner),
        out_shape=[jax.ShapeDtypeStruct(shape, t) for t in (jnp.bfloat16,) * 3 + (jnp.float32,)],
        grid=(half + 1,),
        in_specs=[vmem] * 5 + [table] * 4,
        out_specs=[vmem] * 4,
        scratch_shapes=[
            pltpu.VMEM((half + 1, 2 * inner, 3 * full), jnp.bfloat16),
            pltpu.VMEM((half + 1, 2 * inner, 3 * full), jnp.bfloat16),
            pltpu.VMEM((half + 1, 2 * inner, 3 * full), jnp.float32),
        ],
        compiler_params=pltpu.CompilerParams(vmem_limit_bytes=(58 if pad else 40) * 2**20),
    )(values, gates, grads, filters, skips, *(jnp.asarray(t) for t in tables(length)))
    return [x[:, :width] for x in outs] if pad else outs


def fused_kernel(outer, inner, n_dp, n_ctx, v_in, g_in, o_in, f_in, s_ref, fh_in, fl_in, ih_in, il_in,
                 mixed_out, ggate_out, gval_out, gfil_out,
                 v_ref, g_ref, o_ref, f_ref, fh, fl, ih, il, ahi, alo, spec, back,
                 mixed_ref, ggate_ref, gval_ref, gfil_ref, x_buf, z_buf, sum_ref,
                 tab_sem, own_sem, in_send, in_recv, out_send, out_recv,
                 x_send, x_recv, z_send, z_recv, pc_send, pc_recv, ag_send, fw_send, ag_recv):
    half = outer // 2
    length, width = v_ref.shape
    rows_here = length // n_ctx
    rows_piece = length // n_dp
    dp, ctx = lax.axis_index("dp"), lax.axis_index("context")
    f32 = jnp.float32
    dot = partial(jnp.dot, preferred_element_type=f32)

    def ctx_at(step):
        return lax.rem(ctx + step + n_ctx, n_ctx)

    n_z = n_dp // 2
    z, x = dp // 2, lax.rem(dp, 2)
    across = 2 * z + 1 - x

    def z_at(step):
        return lax.rem(z + step + n_z, n_z)

    def block_rows(p):
        return pl.ds(pl.multiple_of(p * rows_here, 16), rows_here)

    def block_cols(p):
        return pl.ds(pl.multiple_of(p * width, LANES), width)

    loads = [
        pltpu.make_async_copy(src, dst, tab_sem.at[i])
        for i, (src, dst) in enumerate(((fh_in, fh), (fl_in, fl), (ih_in, ih), (il_in, il)))
    ]
    arrays = ((v_in, v_ref), (g_in, g_ref), (o_in, o_ref), (f_in, f_ref))
    own = [
        pltpu.make_async_copy(src.at[:, block_cols(ctx)], dst.at[block_rows(ctx), :], own_sem.at[i])
        for i, (src, dst) in enumerate(arrays)
    ]
    for copy in own + loads:
        copy.start()

    barrier = pltpu.get_barrier_semaphore()
    for step in range(1, n_ctx):
        pl.semaphore_signal(barrier, inc=1, device_id={"context": ctx_at(step)}, device_id_type=MESH)
    pl.semaphore_signal(barrier, inc=1, device_id={"dp": across}, device_id_type=MESH)
    for step in range(1, n_z):
        pl.semaphore_signal(barrier, inc=1, device_id={"dp": 2 * z_at(step) + x}, device_id_type=MESH)
    pl.semaphore_wait(barrier, n_ctx - 1 + 1 + n_z - 1)

    def inbound(i, step):
        src, dst = arrays[i]
        return pltpu.make_async_remote_copy(
            src_ref=src.at[:, block_cols(ctx_at(step))],
            dst_ref=dst.at[block_rows(ctx_at(-step)), :],
            send_sem=in_send.at[i, step],
            recv_sem=in_recv.at[i, step],
            device_id={"context": ctx_at(step)},
            device_id_type=MESH,
        )

    def outbound_in(i, step):
        src, dst = arrays[i]
        return pltpu.make_async_remote_copy(
            src_ref=src.at[:, block_cols(ctx_at(step))],
            dst_ref=dst.at[block_rows(ctx), :],
            send_sem=in_send.at[i, step],
            recv_sem=in_recv.at[i, step],
            device_id={"context": ctx_at(step)},
            device_id_type=MESH,
        )

    for i in range(3):
        for step in range(1, n_ctx):
            outbound_in(i, step).start()

    def arrived(i):
        own[i].wait()
        for step in range(1, n_ctx):
            inbound(i, step).wait_recv()

    def take(ref, a, row):
        return ref[pl.ds(pl.multiple_of(a * inner + row, STRIP), STRIP), :].astype(f32)

    def spread(which, blocks, row):
        cols = pl.ds(which * width, width)
        for freq, (re, im) in enumerate(real_dft(blocks + [None] * half)):
            split_store(ahi, alo, (freq, pl.ds(row, STRIP), cols), re)
            im = jnp.zeros_like(re) if im is None else im
            split_store(ahi, alo, (freq, pl.ds(pl.multiple_of(inner + row, STRIP), STRIP), cols), im)

    def gather(which, row):
        cols = pl.ds(which * width, width)
        hs = []
        for freq in range(half + 1):
            re = back[freq, pl.ds(row, STRIP), cols]
            if freq in (0, half):
                hs.append((re, None))
            else:
                hs.append((re, back[freq, pl.ds(pl.multiple_of(inner + row, STRIP), STRIP), cols]))
        return real_inverse(hs)

    def strips(body):
        def run(strip, carry):
            body(pl.multiple_of(strip * STRIP, STRIP))
            return carry

        lax.fori_loop(0, inner // STRIP, run, 0)

    def invert(k, which, re, im):
        hi, lo = split(jnp.concatenate([re, im], 0))
        back[k, :, pl.ds(which * width, width)] = dot3(ih[k], il[k], hi, lo)

    arrived(0)

    def spread_values(row):
        spread(0, [take(v_ref, a, row) for a in range(half)], row)

    strips(spread_values)
    arrived(1)
    arrived(2)
    for step in range(1, n_ctx):
        outbound_in(3, step).start()

    def spread_grads(row):
        spread(1, [take(g_ref, a, row) * take(o_ref, a, row) for a in range(half)], row)

    strips(spread_grads)
    for copy in loads:
        copy.wait()

    def first(k, carry):
        both = dot3(fh[k], fl[k], ahi[k, :, : 2 * width], alo[k, :, : 2 * width])
        spec[k] = both
        vr, gr = both[:inner, :width], both[:inner, width:]
        vi, gi = both[inner:, :width], both[inner:, width:]
        invert(k, 2, gr * vr + gi * vi, gi * vr - gr * vi)
        return carry

    lax.fori_loop(0, half + 1, first, 0)

    def gather_filters(row):
        for a, conv in enumerate(gather(2, row)):
            gfil_ref[pl.ds(pl.multiple_of(a * inner + row, STRIP), STRIP), :] = conv

    strips(gather_filters)

    def piece_rows(d):
        place = lax.rem(d, n_ctx) * (n_dp // n_ctx) + d // n_ctx
        return pl.ds(pl.multiple_of(place * rows_piece, 8), rows_piece)

    cross = {
        step: pltpu.make_async_remote_copy(
            src_ref=gfil_ref.at[piece_rows(2 * z_at(step) + 1 - x), :],
            dst_ref=x_buf.at[step],
            send_sem=x_send.at[step],
            recv_sem=x_recv.at[step],
            device_id={"dp": across},
            device_id_type=MESH,
        )
        for step in range(n_z)
    }
    order = sorted(range(1, n_z), key=lambda step: abs(step - n_z // 2)) + [0]
    for step in order:
        cross[step].start()
    along = {
        step: pltpu.make_async_remote_copy(
            src_ref=x_buf.at[step],
            dst_ref=z_buf.at[step],
            send_sem=z_send.at[step],
            recv_sem=z_recv.at[step],
            device_id={"dp": 2 * z_at(step) + x},
            device_id_type=MESH,
        )
        for step in range(1, n_z)
    }

    arrived(3)

    def spread_filters(row):
        spread(2, [take(f_ref, a, row) for a in range(half)], row)

    strips(spread_filters)

    def second(k, carry):
        filt = dot3(fh[k], fl[k], ahi[k, :, 2 * width:], alo[k, :, 2 * width:])
        fr, fi = filt[:inner], filt[inner:]
        both = spec[k]
        vr, gr = both[:inner, :width], both[:inner, width:]
        vi, gi = both[inner:, :width], both[inner:, width:]
        invert(k, 0, vr * fr - vi * fi, vr * fi + vi * fr)
        invert(k, 1, gr * fr + gi * fi, gi * fr - gr * fi)
        return carry

    middle = (half + 1) // 2
    lax.fori_loop(0, middle, second, 0)
    for step in order[:-1]:
        cross[step].wait_recv()
        x_buf[step] = x_buf[step] + gfil_ref[piece_rows(2 * z_at(step) + x), :]
        along[step].start()
    lax.fori_loop(middle, half + 1, second, 0)
    skip = s_ref[...]

    def finish(row):
        def rows(a):
            return pl.ds(pl.multiple_of(a * inner + row, STRIP), STRIP)

        for a, conv in enumerate(gather(0, row)):
            gate, grad = take(g_ref, a, row), take(o_ref, a, row)
            mixer = conv + skip * take(v_ref, a, row)
            mixed_ref[rows(a), :] = (gate * mixer).astype(jnp.bfloat16)
            ggate_ref[rows(a), :] = (grad * mixer).astype(jnp.bfloat16)
        for a, conv in enumerate(gather(1, row)):
            gm = take(g_ref, a, row) * take(o_ref, a, row)
            gval_ref[rows(a), :] = (conv + skip * gm).astype(jnp.bfloat16)


    cross[0].wait_recv()
    total = gfil_ref[piece_rows(dp), :] + x_buf[0]
    for step in range(1, n_z):
        along[step].wait_recv()
        total = total + z_buf[step]
    sum_ref[...] = total

    holder = lax.rem(dp, n_ctx)
    part = dp // n_ctx
    gap = lax.rem(ctx - holder + n_ctx, n_ctx)

    def part_of(j, c):
        return gfil_out.at[pl.ds(pl.multiple_of(j * rows_piece, 8), rows_piece), block_cols(c)]

    def collect(which, c):
        return pltpu.make_async_remote_copy(
            src_ref=sum_ref,
            dst_ref=part_of(part, c),
            send_sem=pc_send.at[which],
            recv_sem=pc_recv.at[which],
            device_id={"context": holder},
            device_id_type=MESH,
        )

    def relay(j, c, target, sem):
        return pltpu.make_async_remote_copy(
            src_ref=part_of(j, c),
            dst_ref=part_of(j, c),
            send_sem=sem,
            recv_sem=ag_recv.at[j, c],
            device_id={"dp": target},
            device_id_type=MESH,
        )

    def onward(step, c):
        return relay(part, c, 2 * z_at(step) + x, ag_send.at[step, c])

    def sideways(j, c):
        return relay(j, c, across, fw_send.at[j, c])

    @pl.when(ctx != holder)
    def _():
        collect(gap, ctx).start()

    strips(finish)
    results = ((mixed_ref, mixed_out), (ggate_ref, ggate_out), (gval_ref, gval_out))

    def returned(i, step, landing):
        src, dst = results[i]
        return pltpu.make_async_remote_copy(
            src_ref=src.at[block_rows(ctx_at(step)), :],
            dst_ref=dst.at[:, block_cols(landing)],
            send_sem=out_send.at[i, step],
            recv_sem=out_recv.at[i, step],
            device_id={"context": ctx_at(step)},
            device_id_type=MESH,
        )

    for i in range(3):
        for step in range(1, n_ctx):
            returned(i, step, ctx).start()
    kept = [
        pltpu.make_async_copy(src.at[block_rows(ctx), :], dst.at[:, block_cols(ctx)], own_sem.at[i])
        for i, (src, dst) in enumerate(results)
    ]
    for copy in kept:
        copy.start()

    @pl.when(ctx == holder)
    def _():
        mine = pltpu.make_async_copy(sum_ref, part_of(part, ctx), own_sem.at[3])
        mine.start()
        mine.wait()
        for gap_here in range(n_ctx):
            c = ctx_at(gap_here)
            if gap_here:
                collect(gap_here, c).wait_recv()
            for step in order[:-1]:
                onward(step, c).start()
            sideways(part, c).start()

    parts = n_dp // n_ctx
    relays = []
    for j in range(parts):
        source = ctx + j * n_ctx
        relays.append(jnp.logical_and(lax.rem(source, 2) == x, source != dp))

    for gap_here in range(n_ctx):
        for j in range(parts):
            c = lax.rem(ctx + gap_here, n_ctx)

            @pl.when(relays[j])
            def _():
                sideways(j, c).wait_recv()
                sideways(j, c).start()

    for j in range(parts):
        @pl.when(lax.rem(ctx + j * n_ctx, 2) != x)
        def _():
            for c in range(n_ctx):
                sideways(j, c).wait_recv()

        @pl.when(lax.rem(ctx + j * n_ctx, 2) == x)
        def _():
            for c in range(n_ctx):
                sideways(j, c).wait_send()

    @pl.when(ctx == holder)
    def _():
        for gap_here in range(n_ctx):
            for step in order[:-1]:
                onward(step, ctx_at(gap_here)).wait_send()

    @pl.when(ctx != holder)
    def _():
        collect(gap, ctx).wait_send()

    for copy in kept:
        copy.wait()
    for i in range(3):
        for step in range(1, n_ctx):
            returned(i, step, ctx_at(-step)).wait_recv()
            returned(i, step, ctx).wait_send()
    for i in range(4):
        for step in range(1, n_ctx):
            outbound_in(i, step).wait_send()
    for step in range(n_z):
        cross[step].wait_send()
    for step in range(1, n_z):
        along[step].wait_send()


def hand_over_kernel(*refs):
    count = len(refs) // 2
    for src, dst in zip(refs[:count], refs[count:]):
        dst[...] = src[...]


def hand_over(arrays):
    vmem = pl.BlockSpec(memory_space=pltpu.VMEM)
    return pl.pallas_call(
        hand_over_kernel,
        out_shape=[jax.ShapeDtypeStruct(x.shape, x.dtype) for x in arrays],
        in_specs=[vmem] * len(arrays),
        out_specs=[vmem] * len(arrays),
    )(*arrays)


def fused(values, gates, grads, filters, skips, n_dp, n_ctx):
    rows, columns = values.shape
    length, width = rows * n_ctx, columns // n_ctx
    outer, inner = plan(length)
    half = outer // 2
    vmem = pl.BlockSpec(memory_space=pltpu.VMEM)
    anywhere = pl.BlockSpec(memory_space=pl.ANY)
    bf16, f32 = jnp.bfloat16, jnp.float32
    full = (length, width)
    mats = (half + 1, 2 * inner, 2 * inner)
    rows_piece = length // n_dp
    dma = pltpu.SemaphoreType.DMA
    return pl.pallas_call(
        partial(fused_kernel, outer, inner, n_dp, n_ctx),
        out_shape=[jax.ShapeDtypeStruct((rows, columns), t) for t in (bf16, bf16, bf16, f32)],
        in_specs=[anywhere] * 4 + [vmem] + [anywhere] * 4,
        out_specs=[anywhere] * 4,
        scratch_shapes=[pltpu.VMEM(full, t) for t in (bf16, bf16, bf16, f32)]
        + [pltpu.VMEM(mats, bf16)] * 4
        + [
            pltpu.VMEM((half + 1, 2 * inner, 3 * width), bf16),
            pltpu.VMEM((half + 1, 2 * inner, 3 * width), bf16),
            pltpu.VMEM((half + 1, 2 * inner, 2 * width), f32),
            pltpu.VMEM((half + 1, 2 * inner, 3 * width), f32),
        ]
        + [pltpu.VMEM(full, t) for t in (bf16, bf16, bf16, f32)]
        + [
            pltpu.VMEM((n_dp // 2, rows_piece, width), f32),
            pltpu.VMEM((n_dp // 2, rows_piece, width), f32),
            pltpu.VMEM((rows_piece, width), f32),
            dma((4,)), dma((4,)), dma((4, n_ctx)), dma((4, n_ctx)), dma((3, n_ctx)), dma((3, n_ctx)),
            dma((n_dp // 2,)), dma((n_dp // 2,)), dma((n_dp // 2,)), dma((n_dp // 2,)),
            dma((n_ctx,)), dma((n_ctx,)),
            dma((n_dp // 2, n_ctx)), dma((n_dp // n_ctx, n_ctx)), dma((n_dp // n_ctx, n_ctx)),
        ],
        compiler_params=pltpu.CompilerParams(
            collective_id=0, has_side_effects=True, vmem_limit_bytes=60 * 2**20
        ),
    )(values, gates, grads, filters, skips, *(jnp.asarray(t) for t in tables(length)))


def on_device(values, gates, filters, skips, grad_out):
    rows, columns = values.shape
    group = lax.axis_size("context")
    width = columns // group
    to_channels = partial(lax.all_to_all, axis_name="context", split_axis=1, concat_axis=0, tiled=True)
    to_rows = partial(lax.all_to_all, axis_name="context", split_axis=0, concat_axis=1, tiled=True)
    mine = lax.dynamic_slice_in_dim(skips, lax.axis_index("context") * width, width, 0)
    n_dp = lax.axis_size("dp")
    if width % LANES == 0 and n_dp % group == 0 and n_dp % 2 == 0 and group % 2 == 0:
        return tuple(hand_over(fused(values, gates, grad_out, filters, mine[None, :], n_dp, group)))
    mixed, ggate, gval, gfil = local_mix(
        to_channels(values), to_channels(gates), to_channels(grad_out), to_channels(filters), mine[None, :]
    )
    return to_rows(mixed), to_rows(ggate), to_rows(gval), to_rows(lax.psum(gfil, "dp"))


def solution(mesh):
    placed = (P("context", "dp"), P("context", "dp"), P("context", None), P("dp"), P("context", "dp"))
    return jax.shard_map(
        on_device,
        mesh=mesh,
        in_specs=placed,
        out_specs=(P("context", "dp"), P("context", "dp"), P("context", "dp"), P("context", None)),
        check_vma=False,
    )
```
